256 devices in a mesh: blk: 16 (over x_hi, y, core), grp: 16 (over x_lo, z).
Axes of the slice: x: 4 (x_hi: 2, x_lo: 2; x = x_hi * 2 + x_lo), y: 4, z: 8, core: 2. Of those that a mesh axis runs over, the one named last changes fastest.
Arguments:
- features: bfloat16 [16, 16, 640, 256], P('blk', 'grp'), may hold values from -6 to 6
- tiles: bfloat16 [16, 16, 8, 640, 640], P('blk', 'grp'), as said below
- slot_columns: int32 [16, 16, 8], P('blk', 'grp'), may hold values from 0 to 15, as said below
- slot_counts: int32 [16, 16], P('blk', 'grp'), may hold values from 2 to 8, as said below
- weight: bfloat16 [256, 256], replicated, may hold values from -0.375 to 0.375
- out_grad: bfloat16 [16, 16, 640, 256], P('blk', 'grp'), may hold values from -6 to 6
Outputs:
- layer_output: bfloat16 [16, 16, 640, 256], P('blk', 'grp')
- feature_grad: bfloat16 [16, 16, 640, 256], P('blk', 'grp')
- weight_grad: float32 [256, 256], replicated
The draws below stay inside these ranges and needn't reach their ends.
Inputs may be any that keep to these rules, and one draw needn't show every extreme that they name: `slot_columns`: slot 0 of row block b names b itself; the next slot_counts - 1 slots name distinct other blocks of the same graph in ascending order; unused slots name b. The block pattern is symmetric: row block b names c exactly when row block c names b. `slot_counts`: in every graph one row block uses all 8 slots. `tiles`: for active slots: when row block b names c != b, the tile of row block c that names b is the transpose of b's tile; the tile of slot 0 is symmetric.
All inputs are finite; a program needn't handle non-finite values.
Results may differ from the reference program's by a relative error of at most 0.015.
Values may be sent and summed in bfloat16 or wider, within the bound.
A program may use at most 64 MiB of HBM per device.

```python
import math
import jax
import jax.numpy as jnp
from jax import lax

F = 256
H = 256
R = 640
SLOTS = 8
BLOCKS = 16
GRAPHS = 16
NODES = 163840


def block_pattern(key):
    base_key = jax.random.fold_in(key, 11)
    block_ids = jnp.arange(BLOCKS, dtype=jnp.int32)
    slot_ids = jnp.arange(SLOTS - 1, dtype=jnp.int32)

    def one_graph(graph_id):
        order = jax.random.permutation(jax.random.fold_in(base_key, graph_id), BLOCKS)
        ranks = jnp.argsort(order, stable=True).astype(jnp.int32)
        lower = jnp.minimum(ranks[:, None], ranks[None, :])
        upper = jnp.maximum(ranks[:, None], ranks[None, :])
        linked = (lower != upper) & ((lower + upper <= SLOTS - 1) | (upper == lower + 1))
        sort_keys = jnp.where(linked, block_ids[None, :], BLOCKS + block_ids[None, :])
        ranked = jnp.sort(sort_keys, axis=1)[:, :SLOTS - 1]
        degree = jnp.sum(linked.astype(jnp.int32), axis=1).astype(jnp.int32)
        others = jnp.where(slot_ids[None, :] < degree[:, None], ranked, block_ids[:, None])
        columns = jnp.concatenate([block_ids[:, None], others], axis=1).astype(jnp.int32)
        return (columns, degree + 1)
    columns, counts = jax.vmap(one_graph)(jnp.arange(GRAPHS, dtype=jnp.int32))
    return (jnp.transpose(columns, (1, 0, 2)), jnp.transpose(counts, (1, 0)))


def draw_slot_columns(key, part):
    return block_pattern(key)[0]


def draw_slot_counts(key, part):
    return block_pattern(key)[1]


def draw_tiles(key, part):
    columns, counts = block_pattern(key)
    tile_key = jax.random.fold_in(key, 23)
    scale_factor = 0.5 / math.sqrt(R)

    def one_slot(block_id, graph_id, slot_id):
        column = columns[block_id, graph_id, slot_id]
        lower = jnp.minimum(block_id, column)
        upper = jnp.maximum(block_id, column)
        active = slot_id < counts[block_id, graph_id]
        pair_id = (graph_id * BLOCKS + lower) * BLOCKS + upper
        spare_id = GRAPHS * BLOCKS * BLOCKS + (graph_id * BLOCKS + block_id) * SLOTS + slot_id
        sub_key = jax.random.fold_in(tile_key, jnp.where(active, pair_id, spare_id))
        values = jax.random.normal(sub_key, (R, R), jnp.float32)
        flipped = values.T
        symmetric = (values + flipped) * 0.70710678
        chosen = jnp.where(block_id == column, symmetric, jnp.where(block_id > column, flipped, values))
        return (chosen * scale_factor).astype(jnp.bfloat16)

    def one_row(block_id):
        graph_ids = jnp.arange(GRAPHS, dtype=jnp.int32)
        slot_ids = jnp.arange(SLOTS, dtype=jnp.int32)
        inner = jax.vmap(lambda graph_id, slot_id: one_slot(block_id, graph_id, slot_id), in_axes=(None, 0))
        return jax.vmap(inner, in_axes=(0, None))(graph_ids, slot_ids)
    return lax.map(one_row, jnp.arange(BLOCKS, dtype=jnp.int32))


def steps_of(rng, shape, cuts, smallest, largest):
    def one(axis_at, parts):
        draws = jax.random.uniform(jax.random.fold_in(jax.random.fold_in(rng, 6), axis_at), (parts,), jnp.float32, smallest / len(cuts), largest / len(cuts))
        return jnp.repeat(jnp.exp(draws), shape[axis_at] // parts).reshape((-1,) + (1,) * (len(shape) - axis_at - 1))

    loudness = one(*cuts[0])
    for cut in cuts[1:]:
        loudness = loudness * one(*cut)
    return loudness


def gaussian(stream_key, extent, width, bound, split=(), kind=jnp.bfloat16):
    entries = width * jax.random.normal(stream_key, extent, jnp.float32)
    if split:
        entries = entries * steps_of(stream_key, extent, split, -0.22, 0.18)
    return jnp.clip(entries, -bound, bound).astype(kind)


def setup_inputs(seed: int = 0) -> dict:
    seeds = jax.random.split(jax.random.key(seed), 7)
    return {
        "features": gaussian(seeds[0], (BLOCKS, GRAPHS, R, F), 1.0, 6.0, ((0, 16), (1, 16))),
        "tiles": draw_tiles(jax.random.fold_in(seeds[6], 71), 0),
        "slot_columns": draw_slot_columns(jax.random.fold_in(seeds[6], 71), 0),
        "slot_counts": draw_slot_counts(jax.random.fold_in(seeds[6], 71), 0),
        "weight": gaussian(seeds[4], (F, H), F ** -0.5, 0.375),
        "out_grad": gaussian(seeds[5], (BLOCKS, GRAPHS, R, H), 1.0, 6.0, ((0, 16), (1, 16))),
    }


def silu_slope(linear):
    sigmoid_v = jax.nn.sigmoid(linear)
    return sigmoid_v * (1.0 + linear * (1.0 - sigmoid_v))

def reference(features, tiles, slot_columns, slot_counts, weight, out_grad):
    slot_ids = jnp.arange(SLOTS, dtype=jnp.int32)
    block_ids = jnp.arange(BLOCKS, dtype=jnp.int32)

    def one_graph(graph_id):
        node_feats = features[:, graph_id].astype(jnp.float32)
        blocks = tiles[:, graph_id].astype(jnp.float32)
        columns = slot_columns[:, graph_id].astype(jnp.int32)
        active = (slot_ids[None, :] < slot_counts[:, graph_id][:, None]).astype(jnp.float32)
        masked = blocks * active[:, :, None, None]
        picked = node_feats[columns]
        gathered = jnp.einsum('bkrs,bksf->brf', masked, picked)
        summed = gathered.astype(jnp.bfloat16).reshape(BLOCKS * R, F)
        linear = jnp.dot(summed, weight, preferred_element_type=jnp.float32)
        output = jax.nn.silu(linear).astype(jnp.bfloat16)
        cotangent = out_grad[:, graph_id].reshape(BLOCKS * R, H).astype(jnp.float32)
        slope_grad = (cotangent * silu_slope(linear)).astype(jnp.bfloat16)
        partial_value = jnp.dot(summed.T, slope_grad, preferred_element_type=jnp.float32)
        panel_grad = jnp.dot(slope_grad, weight.T, preferred_element_type=jnp.float32).astype(jnp.bfloat16)
        panel_grad = panel_grad.reshape(BLOCKS, R, F).astype(jnp.float32)
        products = jnp.einsum('bkrs,brf->bksf', masked, panel_grad)
        onehot = (columns[:, :, None] == block_ids[None, None, :]).astype(jnp.float32)
        grads = jnp.einsum('bkc,bksf->csf', onehot, products).astype(jnp.bfloat16)
        return (output.reshape(BLOCKS, R, H), grads, partial_value)
    outputs, grads, partials = lax.map(one_graph, jnp.arange(GRAPHS, dtype=jnp.int32))
    layer_output = jnp.transpose(outputs, (1, 0, 2, 3))
    feature_grad = jnp.transpose(grads, (1, 0, 2, 3))
    weight_grad = lax.optimization_barrier(jnp.sum(partials, axis=0)) * (1.0 / math.sqrt(NODES))
    return (layer_output, feature_grad, weight_grad)
```

```python
import functools
import math

import jax
import jax.numpy as jnp
from jax import lax
from jax.experimental import pallas as pl
from jax.experimental.pallas import tpu as pltpu
from jax.sharding import PartitionSpec as P

ROWS = 640
WIDTH = 256
SLOTS = 8
CHUNK = 128
CHUNKS = ROWS // CHUNK

ORDER = ((0, 0), (0, 3), (0, 1), (1, 0), (0, 2), (1, 2), (1, 3), (1, 1))
OWN, YM, YP, PX, Y2, PY2, PYM, PYP = range(8)


def place():
    b = lax.axis_index("blk")
    g = lax.axis_index("grp")
    return (b // 8) * 2 + g // 8, (b // 2) % 4, g % 8, b % 2


def device(x, y, z, c):
    return {"blk": (x // 2) * 8 + y * 2 + c, "grp": (x % 2) * 8 + z}


def shifted(dx=0, dy=0, dz=0, dc=0):
    x, y, z, c = place()
    return device((x + dx) % 4, (y + dy) % 4, (z + dz) % 8, (c + dc) % 2)


def gather(buf, recv, twin, sent):
    core = lax.axis_index("blk") % 2

    def rows(q):
        return pl.ds(pl.multiple_of(q * CHUNK, CHUNK), CHUNK)

    def send(src, dst, q, target):
        pltpu.make_async_remote_copy(
            buf.at[2 * src, rows(q)], buf.at[2 * dst, rows(q)], sent, recv.at[dst, q], device_id=target
        ).start()

    def pair(o, q):
        pltpu.make_async_remote_copy(
            buf.at[2 * o, rows(q)], buf.at[2 * o + 1, rows(q)], sent, twin.at[o], device_id=shifted(dc=1)
        ).start()

    def own(q):
        send(OWN, YM, q, shifted(dy=1))
        send(OWN, YP, q, shifted(dy=-1))
        send(OWN, PX, q, shifted(dx=2))
        pair(OWN, q)

    def arrived(o, q):
        pltpu.make_async_copy(buf.at[2 * o, rows(q)], buf.at[2 * o, rows(q)], recv.at[o, q]).wait()

    def first(q):
        up = (q < 2) | ((q == 2) & (core == 0))
        arrived(YM, q)

        @pl.when(up)
        def _():
            send(YM, Y2, q, shifted(dy=1))

        pair(YM, q)
        arrived(YP, q)

        @pl.when(jnp.logical_not(up))
        def _():
            send(YP, Y2, q, shifted(dy=-1))

        pair(YP, q)
        arrived(PX, q)
        send(PX, PYM, q, shifted(dy=1))
        send(PX, PYP, q, shifted(dy=-1))
        pair(PX, q)

    def second(q):
        arrived(Y2, q)
        send(Y2, PY2, q, shifted(dx=2))
        pair(Y2, q)

    def third(q):
        for o in (PY2, PYM, PYP):
            arrived(o, q)
            pair(o, q)

    def twin_arrived(o):
        pltpu.make_async_copy(buf.at[2 * o + 1], buf.at[2 * o + 1], twin.at[o]).wait()

    def drain():
        pltpu.make_async_copy(buf.at[pl.ds(0, 15)], buf.at[pl.ds(0, 15)], sent).wait()

    return own, first, second, third, twin_arrived, drain


def kernel(
    scale,
    kof,
    feat_hbm,
    tiles_hbm,
    weight_hbm,
    og_hbm,
    lo_hbm,
    fg_hbm,
    wg_hbm,
    tiles,
    g1,
    g2,
    acc,
    weight,
    og,
    agg,
    slope,
    lo,
    fg,
    wp,
    r1,
    r2,
    r3,
    r4,
    wo,
    local,
    recv1,
    twin1,
    recv2,
    twin2,
    sent,
    wrecv,
    wsent,
):
    x, y, z, c = place()
    load_f = pltpu.make_async_copy(feat_hbm, g1.at[0], local.at[0])
    load_t = pltpu.make_async_copy(tiles_hbm, tiles.at[pl.ds(0, SLOTS)], local.at[1])
    load_w = pltpu.make_async_copy(weight_hbm, weight, local.at[2])
    load_o = pltpu.make_async_copy(og_hbm, og, local.at[3])
    load_f.start()
    load_t.start()
    load_w.start()
    load_o.start()

    barrier = pltpu.get_barrier_semaphore()
    peers = [shifted(dc=1)]
    peers += [shifted(dy=d) for d in (1, 2, 3)]
    peers += [shifted(dx=d) for d in (1, 2, 3)]
    peers += [shifted(dz=d) for d in range(1, 8)]
    for peer in peers:
        pl.semaphore_signal(barrier, 1, device_id=peer)
    tiles[SLOTS] = jnp.zeros((ROWS, ROWS), jnp.bfloat16)
    load_f.wait()
    pl.semaphore_wait(barrier, len(peers))

    own, first, second, third, twin_arrived, drain1 = gather(g1, recv1, twin1, sent.at[0])
    for q in range(CHUNKS):
        own(q)

    def fold(buf, slot):
        acc[...] += jnp.dot(tiles[kof[slot]], buf[slot], preferred_element_type=jnp.float32)

    def run(buf, first, second, third, twin_arrived, hook):
        acc[...] = jnp.dot(tiles[kof[0]], buf[0], preferred_element_type=jnp.float32)

        def a_step(q, carry):
            first(q)
            hook(0, q)
            return carry

        lax.fori_loop(0, CHUNKS, a_step, 0)

        def fold_at(slot):
            @pl.when(slot % 2 == 1)
            def _():
                twin_arrived(slot // 2)

            fold(buf, slot)

        def b_step(q, carry):
            second(q)
            hook(1, q)
            fold_at(1 + q)
            return carry

        lax.fori_loop(0, CHUNKS, b_step, 0)

        def c_step(q, carry):
            third(q)
            hook(2, q)
            fold_at(6 + q)
            return carry

        lax.fori_loop(0, CHUNKS, c_step, 0)

        def d_step(s, carry):
            fold_at(s)
            return carry

        lax.fori_loop(11, 16, d_step, 0)

    load_t.wait()
    run(g1, first, second, third, twin_arrived, lambda phase, q: None)
    load_w.wait()
    load_o.wait()

    own, first, second, third, twin_arrived, drain2 = gather(g2, recv2, twin2, sent.at[1])

    def middle(q, carry):
        rows = pl.ds(pl.multiple_of(q * CHUNK, CHUNK), CHUNK)
        a = acc[rows, :].astype(jnp.bfloat16)
        agg[rows, :] = a
        linear = jnp.dot(a, weight[...], preferred_element_type=jnp.float32)
        sig = jax.nn.sigmoid(linear)
        lo[rows, :] = (linear * sig).astype(jnp.bfloat16)
        s = (og[rows, :].astype(jnp.float32) * (sig * (1.0 + linear * (1.0 - sig)))).astype(jnp.bfloat16)
        slope[rows, :] = s
        g2[0, rows, :] = lax.dot_general(
            s, weight[...], (((1,), (1,)), ((), ())), preferred_element_type=jnp.float32
        ).astype(jnp.bfloat16)
        own(q)
        return carry

    lax.fori_loop(0, CHUNKS, middle, 0)
    store_lo = pltpu.make_async_copy(lo, lo_hbm, local.at[4])
    store_lo.start()
    partial = lax.dot_general(
        agg[...], slope[...], (((0,), (0,)), ((), ())), preferred_element_type=jnp.float32
    )
    wp[...] = partial.reshape(wp.shape)

    def stage(i, ref, n):
        return wrecv.at[i], wsent.at[i]

    def put(i, src, dst, target):
        pltpu.make_async_remote_copy(src, dst, wsent.at[i], wrecv.at[i], device_id=target).start()

    def got(i, ref):
        pltpu.make_async_copy(ref, ref, wrecv.at[i]).wait()

    put(0, wp.at[1 - c], r1, shifted(dc=1))

    def over_z():
        got(0, r1)
        wp[c] = wp[c] + r1[...]
        for d in range(1, 8):
            put(1, wp.at[c, (z + d) % 8], r2.at[d - 1], shifted(dz=d))

    def over_x():
        got(1, r2)
        r3[x] = wp[c, z] + jnp.sum(r2[...], axis=0)
        for d in range(1, 4):
            put(2, r3.at[x], r3.at[x], shifted(dx=d))

    def over_y():
        got(2, r3.at[pl.ds(0, 3)])
        r4[y] = (r3[0] + r3[1]) + (r3[2] + r3[3])
        for d in range(1, 4):
            put(3, r4.at[y], r4.at[y], shifted(dy=d))

    def back_z():
        got(3, r4.at[pl.ds(0, 3)])
        wo[c, z] = ((r4[0] + r4[1]) + (r4[2] + r4[3])) * scale
        for d in range(1, 8):
            put(4, wo.at[c, z], wo.at[c, z], shifted(dz=d))

    def back_core():
        got(4, r2)
        put(5, wo.at[c], wo.at[c], shifted(dc=1))

    hooks = {(0, 1): over_z, (0, 4): over_x, (1, 2): over_y, (1, 4): back_z, (2, 2): back_core}

    def hook(phase, q):
        for (ph, at), f in hooks.items():
            if ph == phase:
                pl.when(q == at)(f)

    run(g2, first, second, third, twin_arrived, hook)
    fg[...] = acc[...].astype(jnp.bfloat16)
    store_fg = pltpu.make_async_copy(fg, fg_hbm, local.at[5])
    store_fg.start()
    got(5, wo.at[1 - c])
    store_wg = pltpu.make_async_copy(wo, wg_hbm, local.at[6])
    store_wg.start()

    drain1()
    drain2()
    for i, ref in enumerate((r1, r2, r3.at[pl.ds(0, 3)], r4.at[pl.ds(0, 3)], r2, wo.at[0])):
        pltpu.make_async_copy(ref, ref, wsent.at[i]).wait()
    store_lo.wait()
    store_fg.wait()
    store_wg.wait()


def per_device(features, tiles, slot_columns, slot_counts, weight, out_grad):
    b = lax.axis_index("blk")
    p, y, c = b // 8, (b // 2) % 4, b % 2
    columns = slot_columns[0, 0]
    count = slot_counts[0, 0]
    blocks = jnp.stack(
        [
            ((p + dp) % 2) * 8 + ((y + dy) % 4) * 2 + (c + dc) % 2
            for dp, dy in ORDER
            for dc in range(2)
        ]
    )
    slots = jnp.arange(SLOTS, dtype=jnp.int32)
    match = (columns[None, :] == blocks[:, None]) & (slots[None, :] < count)
    kof = jnp.min(jnp.where(match, slots[None, :], SLOTS), axis=1).astype(jnp.int32)
    scale = 1.0 / math.sqrt(ROWS * 256)
    bf, f32 = jnp.bfloat16, jnp.float32
    any_spec = pl.BlockSpec(memory_space=pl.ANY)
    dma = pltpu.SemaphoreType.DMA
    lo, fg, wg = pl.pallas_call(
        functools.partial(kernel, scale),
        name="graph_layer",
        out_shape=(
            jax.ShapeDtypeStruct((ROWS, WIDTH), bf),
            jax.ShapeDtypeStruct((ROWS, WIDTH), bf),
            jax.ShapeDtypeStruct((2, 8, 16, WIDTH), f32),
        ),
        in_specs=[pl.BlockSpec(memory_space=pltpu.SMEM)] + [any_spec] * 4,
        out_specs=(any_spec, any_spec, any_spec),
        scratch_shapes=[
            pltpu.VMEM((SLOTS + 1, ROWS, ROWS), bf),
            pltpu.VMEM((16, ROWS, WIDTH), bf),
            pltpu.VMEM((16, ROWS, WIDTH), bf),
            pltpu.VMEM((ROWS, WIDTH), f32),
            pltpu.VMEM((WIDTH, WIDTH), bf),
            pltpu.VMEM((ROWS, WIDTH), bf),
            pltpu.VMEM((ROWS, WIDTH), bf),
            pltpu.VMEM((ROWS, WIDTH), bf),
            pltpu.VMEM((ROWS, WIDTH), bf),
            pltpu.VMEM((ROWS, WIDTH), bf),
            pltpu.VMEM((2, 8, 16, WIDTH), f32),
            pltpu.VMEM((8, 16, WIDTH), f32),
            pltpu.VMEM((7, 16, WIDTH), f32),
            pltpu.VMEM((4, 16, WIDTH), f32),
            pltpu.VMEM((4, 16, WIDTH), f32),
            pltpu.VMEM((2, 8, 16, WIDTH), f32),
            dma((7,)),
            dma((8, CHUNKS)),
            dma((8,)),
            dma((8, CHUNKS)),
            dma((8,)),
            dma((2,)),
            dma((6,)),
            dma((6,)),
        ],
        compiler_params=pltpu.CompilerParams(
            collective_id=0, has_side_effects=True, vmem_limit_bytes=48 << 20
        ),
    )(kof, features[0, 0], tiles[0, 0], weight, out_grad[0, 0])
    return lo[None, None], fg[None, None], wg.reshape(WIDTH, WIDTH)


def solution(mesh):
    in_specs = (
        P("blk", "grp", None, None),
        P("blk", "grp", None, None, None),
        P("blk", "grp", None),
        P("blk", "grp"),
        P(),
        P("blk", "grp", None, None),
    )
    out_specs = (P("blk", "grp", None, None), P("blk", "grp", None, None), P())
    return jax.shard_map(
        per_device, mesh=mesh, in_specs=in_specs, out_specs=out_specs, check_vma=False
    )
```

```python
import functools
import math

import jax
import jax.numpy as jnp
from jax import lax
from jax.experimental import pallas as pl
from jax.experimental.pallas import tpu as pltpu
from jax.sharding import PartitionSpec as P

ROWS = 640
WIDTH = 256
SLOTS = 8
CHUNK = 128
CHUNKS = ROWS // CHUNK
MADE = (0, 4, 1, 3, 2)

ORDER = ((0, 0), (0, 3), (0, 1), (1, 0), (0, 2), (1, 2), (1, 3), (1, 1))
OWN, YM, YP, PX, Y2, PY2, PYM, PYP = range(8)


def place():
    b = lax.axis_index("blk")
    g = lax.axis_index("grp")
    return (b // 8) * 2 + g // 8, (b // 2) % 4, g % 8, b % 2


def device(x, y, z, c):
    return {"blk": (x // 2) * 8 + y * 2 + c, "grp": (x % 2) * 8 + z}


def shifted(dx=0, dy=0, dz=0, dc=0):
    x, y, z, c = place()
    return device((x + dx) % 4, (y + dy) % 4, (z + dz) % 8, (c + dc) % 2)


class Gather:
    def __init__(self, buf, recv, twin, sent):
        self.buf, self.recv, self.twin, self.sent = buf, recv, twin, sent
        self.core = lax.axis_index("blk") % 2

    def send(self, src, dst, q, at, **shift):
        rows = pl.ds(q * CHUNK, CHUNK)
        pltpu.make_async_remote_copy(
            self.buf.at[2 * src, rows],
            self.buf.at[2 * dst, rows],
            self.sent,
            self.recv.at[at],
            device_id=shifted(**shift),
        ).start()

    def pair(self, o, at, *chunks):
        for q in chunks:
            rows = pl.ds(q * CHUNK, CHUNK)
            pltpu.make_async_remote_copy(
                self.buf.at[2 * o, rows],
                self.buf.at[2 * o + 1, rows],
                self.sent,
                self.twin.at[at],
                device_id=shifted(dc=1),
            ).start()

    def wait(self, sem, chunks):
        if chunks <= CHUNKS:
            ref = self.buf.at[0, pl.ds(0, CHUNK * chunks)]
        elif chunks % CHUNKS == 0:
            ref = self.buf.at[pl.ds(0, chunks // CHUNKS)]
        else:
            ref = self.buf.at[pl.ds(0, chunks // 2), pl.ds(0, 2 * CHUNK)]
        pltpu.make_async_copy(ref, ref, sem).wait()

    def got(self, at):
        self.wait(self.recv.at[at], (2, 2, 2, 4, 2, 3, 2, 2, 1, 2, 2, 1, 4, 4, 2)[at])

    def got_twin(self, at):
        self.wait(self.twin.at[at], (5, 4, 6, 2, 3, 5, 4, 1, 4, 4, 2)[at])

    def own(self, step):
        ups, downs = (((0,), ()), ((), (4,)), ((1,), ()), ((), (3,)), ((2, 3, 4), (2, 1, 0)))[step]
        for i in range(3):
            if i < len(ups):
                q = ups[i]
                self.send(OWN, YM, q, min(q, 3), dy=1)
                self.send(OWN, PX, q, 4 if q < 2 else 5, dx=2)
            if i < len(downs):
                q = downs[i]
                self.send(OWN, YP, q, min(4 - q, 3), dy=-1)
        self.pair(OWN, 0, MADE[step])

    def sides(self, i):
        self.got(i)
        if i < 2:
            self.send(YM, Y2, i, 6 + i, dy=1)
            self.send(YP, Y2, 4 - i, 6 + i, dy=-1)
        if i == 0:
            self.send(YM, PYM, 0, 12, dx=2)
            self.send(YP, PYP, 4, 12, dx=2)
        if i == 2:
            pl.when(self.core == 0)(lambda: self.send(YM, Y2, 2, 8, dy=1))
            pl.when(self.core == 1)(lambda: self.send(YP, Y2, 2, 8, dy=-1))
        part = 1 if i < 2 else 2
        ups = (i,) if i < 3 else (3, 4)
        self.pair(YM, part, *ups)
        self.pair(YP, part, *(4 - q for q in ups))

    def across(self, i):
        self.got(4 + i)
        self.pair(PX, 3 + i, *((0, 1), (2, 3, 4))[i])

    def across_on(self, i):
        self.send(PX, PYM, 1 + i, 12 + (1 + i) // 2, dy=1)
        self.send(PX, PYP, 3 - i, 12 + (1 + i) // 2, dy=-1)

    def opposite(self, i):
        self.got(6 + i)
        for q in ((0, 4), (1, 3), (2,))[i]:
            self.send(Y2, PY2, q, 9 + i, dx=2)
            self.pair(Y2, 5, q)

    def far_opposite(self, i):
        self.got(9 + i)
        self.pair(PY2, 6 if i < 2 else 7, *((0, 4), (1, 3), (2,))[i])

    def far_sides(self, i):
        self.got(12 + i)
        self.pair(PYM, 8 + i, *((0, 1), (2, 3), (4,))[i])
        self.pair(PYP, 8 + i, *((4, 3), (2, 1), (0,))[i])

    def drain(self):
        self.wait(self.sent, 75)


def run(net, tiles, kof, acc, hooks):
    buf = net.buf
    hooked = bool(hooks)

    def hook(at):
        if hooked:
            hooks[at]()

    def fold(slot, begin=0, end=CHUNKS):
        span = pl.ds(CHUNK * begin, CHUNK * (end - begin))
        acc[...] += jnp.dot(tiles[kof[slot], :, span], buf[slot, span], preferred_element_type=jnp.float32)

    def fold_twins(o, begin, end):
        def step(slot, carry):
            fold(slot, begin, end)
            return carry

        lax.fori_loop(2 * o, 2 * o + 2, step, 0)

    acc[...] = jnp.dot(tiles[kof[0]], buf[0], preferred_element_type=jnp.float32)
    net.sides(0)
    hook(0)
    net.got_twin(0)
    fold(1)
    net.sides(1)
    fold(2 * YM, 0, 2)
    fold(2 * YP, 3, 5)
    net.sides(2)
    net.across(0)
    net.got_twin(1)
    fold(2 * YM + 1, 0, 2)
    fold(2 * YP + 1, 3, 5)
    net.got_twin(3)
    fold_twins(PX, 0, 2)
    hook(1)
    net.sides(3)
    net.across(1)
    net.across_on(0)
    if not hooked:
        for i in range(1, 4):
            net.across_on(i)
    fold(2 * YM, 2, 5)
    net.opposite(0)
    net.got_twin(2)
    fold(2 * YM + 1, 2, 5)
    fold(2 * YP, 0, 3)
    if hooked:
        hook(2)
        for i in range(1, 4):
            net.across_on(i)
    net.opposite(1)
    fold(2 * YP + 1, 0, 3)
    net.opposite(2)
    net.got_twin(4)
    fold_twins(PX, 2, 5)
    fold(2 * Y2)
    net.far_sides(0)
    net.got_twin(5)
    fold(2 * Y2 + 1)
    net.far_opposite(0)
    hook(3)
    fold(2 * PYM, 0, 2)
    fold(2 * PYP, 3, 5)
    net.got_twin(8)
    fold(2 * PYM + 1, 0, 2)
    fold(2 * PYP + 1, 3, 5)
    net.far_sides(1)
    fold(2 * PYM, 2, 4)
    fold(2 * PYP, 1, 3)
    net.far_opposite(1)
    net.got_twin(9)
    fold(2 * PYM + 1, 2, 4)
    fold(2 * PYP + 1, 1, 3)
    net.far_sides(2)
    fold(2 * PY2, 0, 2)
    net.far_opposite(2)
    hook(4)
    fold(2 * PY2, 3, 5)
    net.got_twin(6)
    fold(2 * PY2 + 1, 0, 2)
    fold(2 * PY2 + 1, 3, 5)

    spans = [(o, pl.ds(q * CHUNK, CHUNK)) for o, q in ((PYM, 4), (PYP, 0), (PY2, 2))]

    def rest(rows, dc):
        a = jnp.concatenate([tiles[kof[2 * o + dc], rows, span] for o, span in spans], axis=1)
        v = jnp.concatenate([buf[2 * o + dc, span] for o, span in spans], axis=0)
        return jnp.dot(a, v, preferred_element_type=jnp.float32)

    acc[...] += rest(pl.ds(0, ROWS), 0)
    net.got_twin(7)
    net.got_twin(10)
    return lambda rows: acc[rows, :] + rest(rows, 1)


def kernel(
    scale,
    columns,
    count,
    feat_hbm,
    tiles_hbm,
    weight_hbm,
    og_hbm,
    lo_hbm,
    fg_hbm,
    wg_hbm,
    kof,
    tiles,
    g1,
    g2,
    acc,
    weight,
    og,
    agg,
    slope,
    lo,
    fg,
    wp,
    wb,
    r1,
    r2,
    r3,
    r4,
    wo,
    local,
    recv1,
    twin1,
    recv2,
    twin2,
    sent,
    wrecv,
    wsent,
):
    x, y, z, c = place()
    load_f = pltpu.make_async_copy(feat_hbm, g1.at[0], local.at[0])
    load_t = pltpu.make_async_copy(tiles_hbm, tiles.at[pl.ds(0, SLOTS)], local.at[1])
    load_w = pltpu.make_async_copy(weight_hbm, weight, local.at[2])
    load_o = pltpu.make_async_copy(og_hbm, og, local.at[2])
    load_f.start()
    barrier = pltpu.get_barrier_semaphore()
    peers = [shifted(dc=1)]
    peers += [shifted(dy=d) for d in (1, 2, 3)]
    peers += [shifted(dx=d) for d in (1, 2, 3)]
    peers += [shifted(dz=d) for d in range(1, 8)]
    for peer in peers:
        pl.semaphore_signal(barrier, 1, device_id=peer)
    load_t.start()
    load_w.start()
    load_o.start()
    pl.semaphore_wait(barrier, len(peers))
    load_f.wait()

    net1 = Gather(g1, recv1, twin1, sent.at[0])
    for step in range(CHUNKS):
        net1.own(step)
    tiles[SLOTS] = jnp.zeros((ROWS, ROWS), jnp.bfloat16)
    for o, (dp, dy) in enumerate(ORDER):
        for dc in range(2):
            block = ((x // 2 + dp) % 2) * 8 + ((y + dy) % 4) * 2 + (c + dc) % 2
            slot = jnp.int32(SLOTS)
            for k in range(SLOTS - 1, -1, -1):
                slot = jnp.where((columns[k] == block) & (k < count[0]), k, slot)
            kof[2 * o + dc] = slot
    load_t.wait()
    total = run(net1, tiles, kof, acc, ())
    pltpu.make_async_copy(acc.at[pl.ds(0, 448)], acc.at[pl.ds(0, 448)], local.at[2]).wait()

    net2 = Gather(g2, recv2, twin2, sent.at[1])
    for step in range(CHUNKS):
        rows = pl.ds(MADE[step] * CHUNK, CHUNK)
        a = total(rows).astype(jnp.bfloat16)
        agg[rows, :] = a
        linear = jnp.dot(a, weight[...], preferred_element_type=jnp.float32)
        sig = jax.nn.sigmoid(linear)
        lo[rows, :] = (linear * sig).astype(jnp.bfloat16)
        s = (og[rows, :].astype(jnp.float32) * (sig * (1.0 + linear * (1.0 - sig)))).astype(jnp.bfloat16)
        slope[rows, :] = s
        g2[0, rows, :] = lax.dot_general(
            s, weight[...], (((1,), (1,)), ((), ())), preferred_element_type=jnp.float32
        ).astype(jnp.bfloat16)
        net2.own(step)

    store_lo = pltpu.make_async_copy(lo, lo_hbm, local.at[0])
    store_lo.start()
    partial = lax.dot_general(
        agg[...], slope[...], (((0,), (0,)), ((), ())), preferred_element_type=jnp.float32
    )
    wp[...] = partial.reshape(wp.shape)

    def put(i, src, dst, target):
        pltpu.make_async_remote_copy(src, dst, wsent.at[0], wrecv.at[i], device_id=target).start()

    def got(i, ref):
        pltpu.make_async_copy(ref, ref, wrecv.at[i]).wait()

    put(0, wp.at[1 - c], r1, shifted(dc=1))

    def over_z():
        got(0, r1)
        wb[...] = (wp[c] + r1[...]).astype(jnp.bfloat16)
        for d in range(1, 8):
            put(1, wb.at[(z + d) % 8], r2.at[d - 1], shifted(dz=d))

    def over_x():
        got(1, r2)
        total = wb[z].astype(jnp.float32) + jnp.sum(r2[...].astype(jnp.float32), axis=0)
        r3[x] = total.astype(jnp.bfloat16)
        for d in range(1, 4):
            put(2, r3.at[x], r3.at[x], shifted(dx=d))

    def four(ref):
        v = ref[...].astype(jnp.float32)
        return (v[0] + v[1]) + (v[2] + v[3])

    def over_y():
        got(2, r3.at[pl.ds(0, 3)])
        r4[y] = four(r3).astype(jnp.bfloat16)
        for d in range(1, 4):
            put(3, r4.at[y], r4.at[y], shifted(dy=d))

    def back_z():
        got(3, r4.at[pl.ds(0, 3)])
        wo[c, z] = (four(r4) * scale).astype(jnp.bfloat16)
        for d in range(1, 8):
            put(4, wo.at[c, z], wo.at[c, z], shifted(dz=d))

    def back_core():
        got(4, r2)
        put(5, wo.at[c], wo.at[c], shifted(dc=1))

    hooks = (over_z, over_x, over_y, back_z, back_core)
    total = run(net2, tiles, kof, acc, hooks)
    for q in range(CHUNKS):
        rows = pl.ds(q * CHUNK, CHUNK)
        fg[rows, :] = total(rows).astype(jnp.bfloat16)
        pltpu.make_async_copy(fg.at[rows], fg_hbm.at[rows], local.at[1]).start()
    got(5, wo.at[1 - c])
    store_wg = pltpu.make_async_copy(wo, wg_hbm, local.at[2])
    store_wg.start()

    net1.drain()
    net2.drain()
    pltpu.make_async_copy(acc.at[pl.ds(0, 352)], acc.at[pl.ds(0, 352)], wsent.at[0]).wait()
    store_lo.wait()
    pltpu.make_async_copy(fg, fg_hbm, local.at[1]).wait()
    store_wg.wait()


def hand_out(lo, fg, wg, lo_out, fg_out, wg_out, blocks, wide, narrow, sems):
    def copy(src, dst, i):
        made = pltpu.make_async_copy(src, dst, sems.at[i])
        made.start()
        return made

    came = [copy(wg, narrow, 0), copy(lo, blocks.at[0], 1), copy(fg, blocks.at[1], 2)]
    came[0].wait()
    wide[...] = narrow[...].astype(jnp.float32)
    gone = [copy(wide, wg_out, 3)]
    came[1].wait()
    gone.append(copy(blocks.at[0], lo_out, 4))
    came[2].wait()
    gone.append(copy(blocks.at[1], fg_out, 5))
    for made in gone:
        made.wait()


def per_device(features, tiles, slot_columns, slot_counts, weight, out_grad):
    scale = 1.0 / math.sqrt(ROWS * 256)
    bf, f32 = jnp.bfloat16, jnp.float32
    any_spec = pl.BlockSpec(memory_space=pl.ANY)
    dma = pltpu.SemaphoreType.DMA
    lo, fg, wg = pl.pallas_call(
        functools.partial(kernel, scale),
        name="graph_layer",
        out_shape=(
            jax.ShapeDtypeStruct((ROWS, WIDTH), bf),
            jax.ShapeDtypeStruct((ROWS, WIDTH), bf),
            jax.ShapeDtypeStruct((2, 8, 16, WIDTH), bf),
        ),
        in_specs=[pl.BlockSpec(memory_space=pltpu.SMEM)] * 2 + [any_spec] * 4,
        out_specs=(any_spec, any_spec, any_spec),
        scratch_shapes=[
            pltpu.SMEM((16,), jnp.int32),
            pltpu.VMEM((SLOTS + 1, ROWS, ROWS), bf),
            pltpu.VMEM((16, ROWS, WIDTH), bf),
            pltpu.VMEM((16, ROWS, WIDTH), bf),
            pltpu.VMEM((ROWS, WIDTH), f32),
            pltpu.VMEM((WIDTH, WIDTH), bf),
            pltpu.VMEM((ROWS, WIDTH), bf),
            pltpu.VMEM((ROWS, WIDTH), bf),
            pltpu.VMEM((ROWS, WIDTH), bf),
            pltpu.VMEM((ROWS, WIDTH), bf),
            pltpu.VMEM((ROWS, WIDTH), bf),
            pltpu.VMEM((2, 8, 16, WIDTH), f32),
            pltpu.VMEM((8, 16, WIDTH), bf),
            pltpu.VMEM((8, 16, WIDTH), f32),
            pltpu.VMEM((7, 16, WIDTH), bf),
            pltpu.VMEM((4, 16, WIDTH), bf),
            pltpu.VMEM((4, 16, WIDTH), bf),
            pltpu.VMEM((2, 8, 16, WIDTH), bf),
            dma((3,)),
            dma((15,)),
            dma((11,)),
            dma((15,)),
            dma((11,)),
            dma((2,)),
            dma((6,)),
            dma((1,)),
        ],
        compiler_params=pltpu.CompilerParams(
            collective_id=0, has_side_effects=True, vmem_limit_bytes=62 << 20
        ),
    )(slot_columns[0, 0], slot_counts[0], features[0, 0], tiles[0, 0], weight, out_grad[0, 0])
    lo, fg, wg = pl.pallas_call(
        hand_out,
        name="hand_out",
        out_shape=(
            jax.ShapeDtypeStruct((ROWS, WIDTH), bf),
            jax.ShapeDtypeStruct((ROWS, WIDTH), bf),
            jax.ShapeDtypeStruct((WIDTH, WIDTH), f32),
        ),
        in_specs=[any_spec] * 3,
        out_specs=(any_spec,) * 3,
        scratch_shapes=[pltpu.VMEM((2, ROWS, WIDTH), bf), pltpu.VMEM((WIDTH, WIDTH), f32), pltpu.VMEM((WIDTH, WIDTH), bf), dma((6,))],
    )(lo, fg, wg.reshape(WIDTH, WIDTH))
    return lo[None, None], fg[None, None], wg


def solution(mesh):
    in_specs = (
        P("blk", "grp", None, None),
        P("blk", "grp", None, None, None),
        P("blk", "grp", None),
        P("blk", "grp"),
        P(),
        P("blk", "grp", None, None),
    )
    out_specs = (P("blk", "grp", None, None), P("blk", "grp", None, None), P())
    return jax.shard_map(
        per_device, mesh=mesh, in_specs=in_specs, out_specs=out_specs, check_vma=False
    )
```

```python
import functools
import math

import jax
import jax.numpy as jnp
from jax import lax
from jax.experimental import pallas as pl
from jax.experimental.pallas import tpu as pltpu
from jax.sharding import PartitionSpec as P

ROWS = 640
WIDTH = 256
SLOTS = 8
CHUNK = 128
CHUNKS = ROWS // CHUNK
MADE = (0, 4, 1, 3, 2)

ORDER = ((0, 0), (0, 3), (0, 1), (1, 0), (0, 2), (1, 2), (1, 3), (1, 1))
OWN, YM, YP, PX, Y2, PY2, PYM, PYP = range(8)


def place():
    b = lax.axis_index("blk")
    g = lax.axis_index("grp")
    return (b // 8) * 2 + g // 8, (b // 2) % 4, g % 8, b % 2


def device(x, y, z, c):
    return {"blk": (x // 2) * 8 + y * 2 + c, "grp": (x % 2) * 8 + z}


def shifted(dx=0, dy=0, dz=0, dc=0):
    x, y, z, c = place()
    return device((x + dx) % 4, (y + dy) % 4, (z + dz) % 8, (c + dc) % 2)


class Gather:
    def __init__(self, buf, recv, twin, sent):
        self.buf, self.recv, self.twin, self.sent = buf, recv, twin, sent
        self.core = lax.axis_index("blk") % 2

    def send(self, src, dst, q, at, **shift):
        rows = pl.ds(q * CHUNK, CHUNK)
        pltpu.make_async_remote_copy(
            self.buf.at[2 * src, rows],
            self.buf.at[2 * dst, rows],
            self.sent,
            self.recv.at[at],
            device_id=shifted(**shift),
        ).start()

    def pair(self, o, at, *chunks):
        for q in chunks:
            rows = pl.ds(q * CHUNK, CHUNK)
            pltpu.make_async_remote_copy(
                self.buf.at[2 * o, rows],
                self.buf.at[2 * o + 1, rows],
                self.sent,
                self.twin.at[at],
                device_id=shifted(dc=1),
            ).start()

    def wait(self, sem, chunks):
        if chunks <= CHUNKS:
            ref = self.buf.at[0, pl.ds(0, CHUNK * chunks)]
        elif chunks % CHUNKS == 0:
            ref = self.buf.at[pl.ds(0, chunks // CHUNKS)]
        else:
            ref = self.buf.at[pl.ds(0, chunks // 2), pl.ds(0, 2 * CHUNK)]
        pltpu.make_async_copy(ref, ref, sem).wait()

    def got(self, at):
        self.wait(self.recv.at[at], (2, 2, 2, 4, 2, 3, 2, 2, 1, 2, 2, 1, 4, 4, 2)[at])

    def got_twin(self, at):
        self.wait(self.twin.at[at], (5, 4, 6, 2, 3, 5, 4, 1, 4, 4, 2)[at])

    def own(self, step):
        ups, downs = (((0,), ()), ((), (4,)), ((1,), ()), ((), (3,)), ((2, 3, 4), (2, 1, 0)))[step]
        for i in range(3):
            if i < len(ups):
                q = ups[i]
                self.send(OWN, YM, q, min(q, 3), dy=1)
                self.send(OWN, PX, q, 4 if q < 2 else 5, dx=2)
            if i < len(downs):
                q = downs[i]
                self.send(OWN, YP, q, min(4 - q, 3), dy=-1)
        self.pair(OWN, 0, MADE[step])

    def sides(self, i):
        self.got(i)
        if i < 2:
            self.send(YM, Y2, i, 6 + i, dy=1)
            self.send(YP, Y2, 4 - i, 6 + i, dy=-1)
        if i == 2:
            pl.when(self.core == 0)(lambda: self.send(YM, Y2, 2, 8, dy=1))
            pl.when(self.core == 1)(lambda: self.send(YP, Y2, 2, 8, dy=-1))
        part = 1 if i < 2 else 2
        ups = (i,) if i < 3 else (3, 4)
        self.pair(YM, part, *ups)
        self.pair(YP, part, *(4 - q for q in ups))

    def early(self, i):
        self.send((YM, YP)[i], (PYM, PYP)[i], (0, 4)[i], 12, dx=2)

    def across(self, i):
        self.got(4 + i)
        self.pair(PX, 3 + i, *((0, 1), (2, 3, 4))[i])

    def across_on(self, i):
        self.send(PX, PYM, 1 + i, 12 + (1 + i) // 2, dy=1)
        self.send(PX, PYP, 3 - i, 12 + (1 + i) // 2, dy=-1)

    def opposite(self, i):
        self.got(6 + i)
        for q in ((0, 4), (1, 3), (2,))[i]:
            self.send(Y2, PY2, q, 9 + i, dx=2)
            self.pair(Y2, 5, q)

    def far_opposite(self, i):
        self.got(9 + i)
        self.pair(PY2, 6 if i < 2 else 7, *((0, 4), (1, 3), (2,))[i])

    def far_sides(self, i):
        self.got(12 + i)
        self.pair(PYM, 8 + i, *((0, 1), (2, 3), (4,))[i])
        self.pair(PYP, 8 + i, *((4, 3), (2, 1), (0,))[i])

    def drain(self):
        self.wait(self.sent, 75)


def run(net, tiles, kof, acc, hooks):
    buf = net.buf
    hooked = bool(hooks)

    def hook(at):
        if hooked:
            hooks[at]()

    def fold(slot, begin=0, end=CHUNKS):
        span = pl.ds(CHUNK * begin, CHUNK * (end - begin))
        acc[...] += jnp.dot(tiles[kof[slot], :, span], buf[slot, span], preferred_element_type=jnp.float32)

    def fold_twins(o, begin, end):
        def step(slot, carry):
            fold(slot, begin, end)
            return carry

        lax.fori_loop(2 * o, 2 * o + 2, step, 0)

    acc[...] = jnp.dot(tiles[kof[0]], buf[0], preferred_element_type=jnp.float32)
    net.sides(0)
    net.early(0)
    net.early(1)
    hook(0)
    net.got_twin(0)
    fold(1)
    net.sides(1)
    fold(2 * YM, 0, 2)
    fold(2 * YP, 3, 5)
    net.sides(2)
    net.across(0)
    net.got_twin(1)
    fold(2 * YM + 1, 0, 2)
    fold(2 * YP + 1, 3, 5)
    if hooked:
        net.got_twin(3)
        fold_twins(PX, 0, 2)
        hook(1)
        net.sides(3)
        net.across(1)
        net.across_on(0)
        fold(2 * YM, 2, 5)
        net.opposite(0)
        net.got_twin(2)
        fold(2 * YM + 1, 2, 5)
        fold(2 * YP, 0, 3)
        hook(2)
        for i in range(1, 4):
            net.across_on(i)
        net.opposite(1)
    else:
        fold(2 * PX, 0, 2)
        net.sides(3)
        net.across(1)
        for i in range(4):
            net.across_on(i)
        net.opposite(0)
        net.got_twin(3)
        fold(2 * PX + 1, 0, 2)
        fold(2 * YM, 2, 5)
        net.got_twin(2)
        fold(2 * YM + 1, 2, 5)
        net.opposite(1)
        fold(2 * YP, 0, 3)
    fold(2 * YP + 1, 0, 3)
    net.opposite(2)
    net.got_twin(4)
    fold_twins(PX, 2, 5)
    fold(2 * Y2)
    net.far_sides(0)
    net.got_twin(5)
    fold(2 * Y2 + 1)
    net.far_opposite(0)
    hook(3)
    fold(2 * PYM, 0, 2)
    fold(2 * PYP, 3, 5)
    net.got_twin(8)
    fold(2 * PYM + 1, 0, 2)
    fold(2 * PYP + 1, 3, 5)
    net.far_sides(1)
    fold(2 * PYM, 2, 4)
    fold(2 * PYP, 1, 3)
    net.far_opposite(1)
    net.got_twin(9)
    fold(2 * PYM + 1, 2, 4)
    fold(2 * PYP + 1, 1, 3)
    net.far_sides(2)
    fold(2 * PY2, 0, 2)
    net.far_opposite(2)
    hook(4)
    fold(2 * PY2, 3, 5)
    net.got_twin(6)
    fold(2 * PY2 + 1, 0, 2)
    fold(2 * PY2 + 1, 3, 5)

    spans = [(o, pl.ds(q * CHUNK, CHUNK)) for o, q in ((PYM, 4), (PYP, 0), (PY2, 2))]

    def rest(rows, dc):
        a = jnp.concatenate([tiles[kof[2 * o + dc], rows, span] for o, span in spans], axis=1)
        v = jnp.concatenate([buf[2 * o + dc, span] for o, span in spans], axis=0)
        return jnp.dot(a, v, preferred_element_type=jnp.float32)

    acc[...] += rest(pl.ds(0, ROWS), 0)
    net.got_twin(7)
    net.got_twin(10)
    return lambda rows: acc[rows, :] + rest(rows, 1)


def kernel(
    scale,
    columns_hbm,
    count_hbm,
    feat_hbm,
    tiles_hbm,
    weight_hbm,
    og_hbm,
    lo_hbm,
    fg_hbm,
    wg_hbm,
    columns,
    count,
    kof,
    tiles,
    g1,
    g2,
    acc,
    weight,
    og,
    lo,
    fg,
    wp,
    wb,
    r1,
    r2,
    r3,
    r4,
    wo,
    local,
    recv1,
    twin1,
    recv2,
    twin2,
    sent,
    wrecv,
    wsent,
):
    x, y, z, c = place()
    load_f = pltpu.make_async_copy(feat_hbm, g1.at[0], local.at[0])
    load_t = pltpu.make_async_copy(tiles_hbm, tiles.at[pl.ds(0, SLOTS)], local.at[1])
    load_w = pltpu.make_async_copy(weight_hbm, weight, local.at[2])
    load_o = pltpu.make_async_copy(og_hbm, og, local.at[2])
    load_f.start()
    barrier = pltpu.get_barrier_semaphore()
    peers = [shifted(dc=1)]
    peers += [shifted(dy=d) for d in (1, 2, 3)]
    peers += [shifted(dx=d) for d in (1, 2, 3)]
    peers += [shifted(dz=d) for d in range(1, 8)]
    for peer in peers:
        pl.semaphore_signal(barrier, 1, device_id=peer)
    load_c = pltpu.make_async_copy(columns_hbm, columns, local.at[3])
    load_n = pltpu.make_async_copy(count_hbm, count, local.at[4])
    load_c.start()
    load_n.start()
    load_t.start()
    load_w.start()
    load_o.start()
    pl.semaphore_wait(barrier, len(peers))
    load_f.wait()

    net1 = Gather(g1, recv1, twin1, sent.at[0])
    for step in range(CHUNKS):
        net1.own(step)
    tiles[SLOTS] = jnp.zeros((ROWS, ROWS), jnp.bfloat16)
    load_c.wait()
    load_n.wait()
    for o, (dp, dy) in enumerate(ORDER):
        for dc in range(2):
            block = ((x // 2 + dp) % 2) * 8 + ((y + dy) % 4) * 2 + (c + dc) % 2
            slot = jnp.int32(SLOTS)
            for k in range(SLOTS - 1, -1, -1):
                slot = jnp.where((columns[0, 0, k] == block) & (k < count[0, 0]), k, slot)
            kof[2 * o + dc] = slot
    load_t.wait()
    total = run(net1, tiles, kof, acc, ())
    pltpu.make_async_copy(acc.at[pl.ds(0, 448)], acc.at[pl.ds(0, 448)], local.at[2]).wait()

    net2 = Gather(g2, recv2, twin2, sent.at[1])
    for step in range(CHUNKS):
        rows = pl.ds(MADE[step] * CHUNK, CHUNK)
        a = total(rows).astype(jnp.bfloat16)
        linear = jnp.dot(a, weight[...], preferred_element_type=jnp.float32)
        sig = jax.nn.sigmoid(linear)
        lo[rows, :] = (linear * sig).astype(jnp.bfloat16)
        s = (og[rows, :].astype(jnp.float32) * (sig * (1.0 + linear * (1.0 - sig)))).astype(jnp.bfloat16)
        g2[0, rows, :] = lax.dot_general(
            s, weight[...], (((1,), (1,)), ((), ())), preferred_element_type=jnp.float32
        ).astype(jnp.bfloat16)
        net2.own(step)
        term = lax.dot_general(a, s, (((0,), (0,)), ((), ())), preferred_element_type=jnp.float32).reshape(wp.shape)
        wp[...] = term if step == 0 else wp[...] + term

    store_lo = pltpu.make_async_copy(lo, lo_hbm, local.at[0])
    store_lo.start()
    def put(i, src, dst, target):
        pltpu.make_async_remote_copy(src, dst, wsent.at[0], wrecv.at[i], device_id=target).start()

    def got(i, ref):
        pltpu.make_async_copy(ref, ref, wrecv.at[i]).wait()

    put(0, wp.at[1 - c], r1, shifted(dc=1))

    def over_z():
        got(0, r1)
        wb[...] = (wp[c] + r1[...]).astype(jnp.bfloat16)
        for d in range(1, 8):
            put(1, wb.at[(z + d) % 8], r2.at[d - 1], shifted(dz=d))

    def over_x():
        got(1, r2)
        total = wb[z].astype(jnp.float32) + jnp.sum(r2[...].astype(jnp.float32), axis=0)
        r3[x] = total.astype(jnp.bfloat16)
        for d in range(1, 4):
            put(2, r3.at[x], r3.at[x], shifted(dx=d))

    def four(ref):
        v = ref[...].astype(jnp.float32)
        return (v[0] + v[1]) + (v[2] + v[3])

    def over_y():
        got(2, r3.at[pl.ds(0, 3)])
        r4[y] = four(r3).astype(jnp.bfloat16)
        for d in range(1, 4):
            put(3, r4.at[y], r4.at[y], shifted(dy=d))

    def back_z():
        got(3, r4.at[pl.ds(0, 3)])
        wo[c, z] = (four(r4) * scale).astype(jnp.bfloat16)
        for d in range(1, 8):
            put(4, wo.at[c, z], wo.at[c, z], shifted(dz=d))

    def back_core():
        got(4, r2)
        put(5, wo.at[c], wo.at[c], shifted(dc=1))

    hooks = (over_z, over_x, over_y, back_z, back_core)
    total = run(net2, tiles, kof, acc, hooks)
    for q in range(CHUNKS):
        rows = pl.ds(q * CHUNK, CHUNK)
        fg[rows, :] = total(rows).astype(jnp.bfloat16)
        pltpu.make_async_copy(fg.at[rows], fg_hbm.at[rows], local.at[1]).start()
    got(5, wo.at[1 - c])
    store_wg = pltpu.make_async_copy(wo, wg_hbm, local.at[2])
    store_wg.start()

    net1.drain()
    net2.drain()
    pltpu.make_async_copy(acc.at[pl.ds(0, 352)], acc.at[pl.ds(0, 352)], wsent.at[0]).wait()
    store_lo.wait()
    pltpu.make_async_copy(fg, fg_hbm, local.at[1]).wait()
    store_wg.wait()


def hand_out(lo, fg, wg, lo_out, fg_out, wg_out, blocks, wide, narrow, sems):
    def copy(src, dst, i):
        made = pltpu.make_async_copy(src, dst, sems.at[i])
        made.start()
        return made

    came = [copy(wg, narrow, 0), copy(lo, blocks.at[0], 1), copy(fg, blocks.at[1], 2)]
    came[0].wait()
    wide[...] = narrow[...].astype(jnp.float32)
    gone = [copy(wide, wg_out, 3)]
    came[1].wait()
    gone.append(copy(blocks.at[0], lo_out, 4))
    came[2].wait()
    gone.append(copy(blocks.at[1], fg_out, 5))
    for made in gone:
        made.wait()


def per_device(features, tiles, slot_columns, slot_counts, weight, out_grad):
    scale = 1.0 / math.sqrt(ROWS * 256)
    bf, f32 = jnp.bfloat16, jnp.float32
    any_spec = pl.BlockSpec(memory_space=pl.ANY)
    dma = pltpu.SemaphoreType.DMA
    lo, fg, wg = pl.pallas_call(
        functools.partial(kernel, scale),
        name="graph_layer",
        out_shape=(
            jax.ShapeDtypeStruct((ROWS, WIDTH), bf),
            jax.ShapeDtypeStruct((ROWS, WIDTH), bf),
            jax.ShapeDtypeStruct((2, 8, 16, WIDTH), bf),
        ),
        in_specs=[any_spec] * 6,
        out_specs=(any_spec, any_spec, any_spec),
        scratch_shapes=[
            pltpu.SMEM((1, 1, SLOTS), jnp.int32),
            pltpu.SMEM((1, 1), jnp.int32),
            pltpu.SMEM((16,), jnp.int32),
            pltpu.VMEM((SLOTS + 1, ROWS, ROWS), bf),
            pltpu.VMEM((16, ROWS, WIDTH), bf),
            pltpu.VMEM((16, ROWS, WIDTH), bf),
            pltpu.VMEM((ROWS, WIDTH), f32),
            pltpu.VMEM((WIDTH, WIDTH), bf),
            pltpu.VMEM((ROWS, WIDTH), bf),
            pltpu.VMEM((ROWS, WIDTH), bf),
            pltpu.VMEM((ROWS, WIDTH), bf),
            pltpu.VMEM((2, 8, 16, WIDTH), f32),
            pltpu.VMEM((8, 16, WIDTH), bf),
            pltpu.VMEM((8, 16, WIDTH), f32),
            pltpu.VMEM((7, 16, WIDTH), bf),
            pltpu.VMEM((4, 16, WIDTH), bf),
            pltpu.VMEM((4, 16, WIDTH), bf),
            pltpu.VMEM((2, 8, 16, WIDTH), bf),
            dma((5,)),
            dma((15,)),
            dma((11,)),
            dma((15,)),
            dma((11,)),
            dma((2,)),
            dma((6,)),
            dma((1,)),
        ],
        compiler_params=pltpu.CompilerParams(
            collective_id=0, has_side_effects=True, vmem_limit_bytes=62 << 20
        ),
    )(slot_columns, slot_counts, features[0, 0], tiles[0, 0], weight, out_grad[0, 0])
    lo, fg, wg = pl.pallas_call(
        hand_out,
        name="hand_out",
        out_shape=(
            jax.ShapeDtypeStruct((ROWS, WIDTH), bf),
            jax.ShapeDtypeStruct((ROWS, WIDTH), bf),
            jax.ShapeDtypeStruct((WIDTH, WIDTH), f32),
        ),
        in_specs=[any_spec] * 3,
        out_specs=(any_spec,) * 3,
        scratch_shapes=[pltpu.VMEM((2, ROWS, WIDTH), bf), pltpu.VMEM((WIDTH, WIDTH), f32), pltpu.VMEM((WIDTH, WIDTH), bf), dma((6,))],
    )(lo, fg, wg.reshape(WIDTH, WIDTH))
    return lo[None, None], fg[None, None], wg


def solution(mesh):
    in_specs = (
        P("blk", "grp", None, None),
        P("blk", "grp", None, None, None),
        P("blk", "grp", None),
        P("blk", "grp"),
        P(),
        P("blk", "grp", None, None),
    )
    out_specs = (P("blk", "grp", None, None), P("blk", "grp", None, None), P())
    return jax.shard_map(
        per_device, mesh=mesh, in_specs=in_specs, out_specs=out_specs, check_vma=False
    )
```
